32 devices in a mesh: tok: 4 (over x, core), exp: 8 (over z, y).
Axes of the slice: x: 2, y: 2, z: 4, core: 2. Of those that a mesh axis runs over, the one named last changes fastest.
Arguments:
- tokens: float32 [3072, 1280], P('tok', 'exp'), may hold values from -6 to 6
- out_grad: float32 [3072, 1280], P('tok', 'exp'), may hold values from -6 to 6
- slot_proj: bfloat16 [1280, 2048], P(None, 'exp'), may hold values from -2 to 2
- weight_in: bfloat16 [8, 1280, 5120], P('exp', None, 'tok'), may hold values from -0.15625 to 0.15625
- weight_out: bfloat16 [8, 5120, 1280], P('exp', 'tok'), may hold values from -0.078125 to 0.078125
- slot_norm: float32 [2048], P('exp'), may hold values from -1 to 6
- token_norm: float32 [3072], P('tok'), may hold values from -1 to 6
Outputs:
- grad_tokens: float32 [3072, 1280], P('tok', 'exp')
- grad_slot_proj: float32 [1280, 2048], P('tok', 'exp')
- grad_weight_in: float32 [8, 1280, 5120], P('exp', None, 'tok')
- grad_weight_out: float32 [8, 5120, 1280], P('exp', 'tok')
The draws below stay inside these ranges and needn't reach their ends.
All inputs are finite; a program needn't handle non-finite values.
Results may differ from the reference program's by a relative error of at most 0.012.
The reference program's roundings to bfloat16 on the way (of `hidden`, `slot_out_half`, `pre_grad` and `slot_in_grad_half`) count: a program that leaves them out, or rounds other values in their place, can miss the bound.
Values may be sent and summed in bfloat16 or wider, within the bound.
No kernel may reach another device: no remote copies, remote signals or barrier semaphores. Data moves between devices by JAX's collectives and lax.ppermute only.
A program may use at most 64 MiB of HBM per device.

```python
import jax
import jax.numpy as jnp
from jax import lax

D = 1280
FF = 5120
SLOTS = 256
TOKENS = 3072
EXPERTS = 8


def draw_tokens(key, part):
    values = jnp.clip(jax.random.normal(key, (TOKENS, D), jnp.float32), -6.0, 6.0)
    return values


def draw_slot_proj(key, part):
    spread = 3.0 / jnp.sqrt(jnp.float32(D))
    values = jnp.clip(jax.random.normal(key, (D, EXPERTS * SLOTS), jnp.float32), -4.0, 4.0)
    return (values * spread).astype(jnp.bfloat16)


def draw_slot_norm(key, part):
    values = jax.random.uniform(key, (EXPERTS * SLOTS,), jnp.float32, 4.0, 6.0)
    return values


def draw_token_norm(key, part):
    values = jax.random.uniform(key, (TOKENS,), jnp.float32, 4.0, 6.0)
    return values


def steps_of(rng, dims, split, smallest, high):
    def one(dim, blocks):
        steps = jax.random.uniform(jax.random.fold_in(jax.random.fold_in(rng, 6), dim), (blocks,), jnp.float32, smallest / len(split), high / len(split))
        return jnp.repeat(jnp.exp(steps), dims[dim] // blocks).reshape((-1,) + (1,) * (len(dims) - dim - 1))

    level = one(*split[0])
    for cut in split[1:]:
        level = level * one(*cut)
    return level


def gaussian(rng, shape, width, bound, shards=(), held_as=jnp.bfloat16):
    values = jax.random.normal(rng, shape, jnp.float32) * width
    if len(shards) > 0:
        values = steps_of(rng, shape, shards, -0.22, 0.18) * values
    return jnp.clip(values, min=-bound, max=bound).astype(held_as)


def setup_inputs(seed: int = 0) -> dict:
    streams_of = jax.random.split(jax.random.key(seed), 8)
    tokens = draw_tokens(jax.random.fold_in(streams_of[7], 71), 0)
    out_grad = gaussian(streams_of[1], (TOKENS, D), 1.0, 6.0, ((0, 4), (1, 8)), jnp.float32)
    slot_proj = draw_slot_proj(jax.random.fold_in(streams_of[7], 71), 0)
    weight_in = gaussian(streams_of[3], (EXPERTS, D, FF), D ** -0.5, 0.15625, ((0, 8), (2, 4)))
    weight_out = gaussian(streams_of[4], (EXPERTS, FF, D), FF ** -0.5, 0.078125, ((0, 8), (1, 4)))
    slot_norm = draw_slot_norm(jax.random.fold_in(streams_of[7], 71), 0)
    token_norm = draw_token_norm(jax.random.fold_in(streams_of[7], 71), 0)
    return {"tokens": tokens, "out_grad": out_grad, "slot_proj": slot_proj, "weight_in": weight_in, "weight_out": weight_out, "slot_norm": slot_norm, "token_norm": token_norm}


GELU_C = 0.7978845608028654


def gelu_parts(pre_act):
    inner = GELU_C * (pre_act + 0.044715 * pre_act ** 3)
    tangent = jnp.tanh(inner)
    value = 0.5 * pre_act * (1.0 + tangent)
    slope = 0.5 * (1.0 + tangent) + 0.5 * pre_act * (1.0 - tangent * tangent) * GELU_C * (1.0 + 3.0 * 0.044715 * pre_act * pre_act)
    return value, slope


def weights_of(tok_half, proj_e, norm_e, token_norm):
    logits = jnp.dot(tok_half, proj_e, preferred_element_type=jnp.float32)
    dispatch = jnp.exp(logits - norm_e[None, :]) / jnp.float32(TOKENS)
    combine = jnp.exp(logits - token_norm[:, None]) / jnp.float32(EXPERTS * SLOTS)
    return dispatch, combine


def reference(tokens, out_grad, slot_proj, weight_in, weight_out, slot_norm, token_norm):
    tok_half = tokens.astype(jnp.bfloat16)
    grad_half = out_grad.astype(jnp.bfloat16)
    proj_stack = slot_proj.reshape(D, EXPERTS, SLOTS).transpose(1, 0, 2)
    norm_stack = slot_norm.reshape(EXPERTS, SLOTS)

    def first_pass(items):
        proj_e, norm_e, win_e, wout_e = items
        dispatch, combine = weights_of(tok_half, proj_e, norm_e, token_norm)
        dispatch_half = dispatch.astype(jnp.bfloat16)
        combine_half = combine.astype(jnp.bfloat16)
        slot_in = jnp.dot(dispatch_half.T, tok_half, preferred_element_type=jnp.float32)
        slot_grad = jnp.dot(combine_half.T, grad_half, preferred_element_type=jnp.float32)
        slot_in_half = slot_in.astype(jnp.bfloat16)
        pre_act = jnp.dot(slot_in_half, win_e, preferred_element_type=jnp.float32)
        gelu_out, gelu_slope = gelu_parts(pre_act)
        hidden = gelu_out.astype(jnp.bfloat16)
        slot_out_half = jnp.dot(hidden, wout_e, preferred_element_type=jnp.float32).astype(jnp.bfloat16)
        slot_grad_half = slot_grad.astype(jnp.bfloat16)
        grad_wout = jnp.dot(hidden.T, slot_grad_half, preferred_element_type=jnp.float32)
        hidden_grad = jnp.dot(slot_grad_half, wout_e.T, preferred_element_type=jnp.float32)
        pre_grad = (hidden_grad * gelu_slope).astype(jnp.bfloat16)
        grad_win = jnp.dot(slot_in_half.T, pre_grad, preferred_element_type=jnp.float32)
        slot_in_grad_half = jnp.dot(pre_grad, win_e.T, preferred_element_type=jnp.float32).astype(jnp.bfloat16)
        comb_grad = jnp.dot(grad_half, slot_out_half.T, preferred_element_type=jnp.float32)
        row_part = jnp.sum(combine * comb_grad, axis=1)
        return grad_win, grad_wout, slot_out_half, slot_in_grad_half, row_part

    grad_weight_in, grad_weight_out, outs_half, ingrads_half, row_parts = lax.map(first_pass, (proj_stack, norm_stack, weight_in, weight_out))
    row_stat = jnp.sum(row_parts, axis=0)

    def second_pass(carry, items):
        proj_e, norm_e, out_half, ingrad_half = items
        dispatch, combine = weights_of(tok_half, proj_e, norm_e, token_norm)
        dispatch_half = dispatch.astype(jnp.bfloat16)
        combine_half = combine.astype(jnp.bfloat16)
        comb_grad = jnp.dot(grad_half, out_half.T, preferred_element_type=jnp.float32)
        disp_grad = jnp.dot(tok_half, ingrad_half.T, preferred_element_type=jnp.float32)
        col_stat = jnp.sum(dispatch_half.astype(jnp.float32) * disp_grad, axis=0)
        disp_part = dispatch * (disp_grad - col_stat[None, :])
        inner_grad = (combine * comb_grad + disp_part).astype(jnp.bfloat16)
        logit_grad = (combine * (comb_grad - row_stat[:, None]) + disp_part).astype(jnp.bfloat16)
        proj_grad = jnp.dot(tok_half.T, logit_grad, preferred_element_type=jnp.float32)
        token_term = jnp.dot(inner_grad, proj_e.T, preferred_element_type=jnp.float32)
        token_term = token_term - row_stat[:, None] * jnp.dot(combine_half, proj_e.T, preferred_element_type=jnp.float32)
        token_term = token_term + jnp.dot(dispatch_half, ingrad_half, preferred_element_type=jnp.float32)
        return carry + token_term, proj_grad

    grad_tokens, proj_grads = lax.scan(second_pass, jnp.zeros((TOKENS, D), jnp.float32), (proj_stack, norm_stack, outs_half, ingrads_half))
    grad_slot_proj = proj_grads.transpose(1, 0, 2).reshape(D, EXPERTS * SLOTS)
    return grad_tokens, grad_slot_proj, grad_weight_in, grad_weight_out
```

```python
import jax
import jax.numpy as jnp
from jax import lax
from jax.sharding import PartitionSpec as P

GELU_C = 0.7978845608028654
BF16 = jnp.bfloat16
F32 = jnp.float32


def gelu_parts(pre_act):
    inner = GELU_C * (pre_act + 0.044715 * pre_act**3)
    tangent = jnp.tanh(inner)
    value = 0.5 * pre_act * (1.0 + tangent)
    slope = 0.5 * (1.0 + tangent) + 0.5 * pre_act * (1.0 - tangent * tangent) * GELU_C * (
        1.0 + 3.0 * 0.044715 * pre_act * pre_act
    )
    return (value, slope)


def swap(x, axis, k):
    n = lax.axis_size(axis)
    return lax.ppermute(x, axis, [(i, i ^ k) for i in range(n)])


def split_of(n):
    bits = n.bit_length() - 1
    return 1 << (bits // 2)


def gather_exp(block):
    n = lax.axis_size("exp")
    inner = split_of(n)
    held = {0: block}
    for ko in range(inner, n, inner):
        held[ko] = swap(block, "exp", ko)
    for ko in range(0, n, inner):
        for ki in range(1, inner):
            held[ko + ki] = swap(held[ko], "exp", ki)
    return [held[k] for k in range(n)]


def scatter_exp(blocks):
    n = lax.axis_size("exp")
    inner = split_of(n)
    sums = {}
    for ko in reversed(range(0, n, inner)):
        total = blocks[ko]
        for ki in range(1, inner):
            total = total + swap(blocks[ko + ki].astype(BF16), "exp", ki).astype(F32)
        sums[ko] = total
    out = sums[0]
    for ko in reversed(range(inner, n, inner)):
        out = out + swap(sums[ko].astype(BF16), "exp", ko).astype(F32)
    return out


def scatter_core(part):
    half = part.shape[0] // 2
    core = lax.axis_index("tok") % 2
    mine = lax.dynamic_slice_in_dim(part, core * half, half, 0)
    other = lax.dynamic_slice_in_dim(part, (1 - core) * half, half, 0)
    return mine + swap(other.astype(BF16), "tok", 1).astype(F32)


def sum_tok(part):
    core = lax.axis_index("tok") % 2
    mine = scatter_core(part)
    sent = mine.astype(BF16)
    for k in range(2, lax.axis_size("tok"), 2):
        mine = mine + swap(sent, "tok", k).astype(F32)
    mine = mine.astype(BF16)
    other = swap(mine, "tok", 1)
    low = jnp.where(core == 0, mine, other)
    high = jnp.where(core == 0, other, mine)
    return jnp.concatenate([low, high], axis=0)


def local(tokens, out_grad, slot_proj, weight_in, weight_out, slot_norm, token_norm):
    n_exp = lax.axis_size("exp")
    n_tok = lax.axis_size("tok")
    me = lax.axis_index("exp")
    rows, feat = tokens.shape
    width = feat * n_exp
    slots = slot_proj.shape[1]
    order = jnp.arange(n_exp) ^ me

    def reorder(x):
        return x.reshape(n_exp, feat, x.shape[1])[order].reshape(x.shape)

    proj_rel = reorder(slot_proj)
    tok_t = jnp.concatenate(gather_exp(tokens.T.astype(BF16)), axis=0)
    grad_t = jnp.concatenate(gather_exp(out_grad.T.astype(BF16)), axis=0)

    def dot(a, b, ca, cb):
        return lax.dot_general(a, b, (((ca,), (cb,)), ((), ())), preferred_element_type=F32)

    logits = dot(proj_rel, tok_t, 0, 0)
    dispatch = jnp.exp(logits - slot_norm[:, None]) / F32(rows * n_tok)
    combine = jnp.exp(logits - token_norm[None, :]) / F32(slots * n_exp)
    dispatch_half = dispatch.astype(BF16)
    combine_half = combine.astype(BF16)
    slot_in_half = sum_tok(dot(tok_t, dispatch_half, 1, 1))
    slot_grad_half = sum_tok(dot(grad_t, combine_half, 1, 1))
    slot_in_c = reorder(slot_in_half)
    slot_grad_c = reorder(slot_grad_half)
    w_in, w_out = weight_in[0], weight_out[0]
    pre_act = dot(slot_in_c, w_in, 0, 0)
    gelu_out, gelu_slope = gelu_parts(pre_act)
    hidden = gelu_out.astype(BF16)
    slot_out = sum_tok(dot(w_out, hidden, 0, 1))
    hidden_grad = dot(slot_grad_c, w_out, 0, 1)
    pre_grad = (hidden_grad * gelu_slope).astype(BF16)
    slot_in_grad = sum_tok(dot(w_in, pre_grad, 1, 1))
    grad_weight_out = dot(hidden, slot_grad_c, 0, 1)[None]
    grad_weight_in = dot(slot_in_c, pre_grad, 1, 0)[None]
    out_rel = reorder(slot_out)
    ingrad_rel = reorder(slot_in_grad)
    comb_grad = dot(out_rel, grad_t, 0, 0)
    row_stat = jnp.sum(combine * comb_grad, axis=0, keepdims=True)
    k = 1
    while k < n_exp:
        row_stat = row_stat + swap(row_stat, "exp", k)
        k *= 2
    disp_grad = dot(ingrad_rel, tok_t, 0, 0)
    col_stat = jnp.sum(slot_in_half.astype(F32) * ingrad_rel.astype(F32), axis=0)
    logit_grad = (combine * (comb_grad - row_stat) + dispatch * (disp_grad - col_stat[:, None])).astype(BF16)
    proj_part = dot(tok_t, logit_grad, 1, 1)
    term = dot(
        jnp.concatenate([proj_rel, ingrad_rel], axis=1),
        jnp.concatenate([logit_grad, dispatch_half], axis=0),
        1,
        0,
    )
    grad_tokens = scatter_exp([term[k * feat : (k + 1) * feat] for k in range(n_exp)]).T

    share = width // n_tok
    proj_part = reorder(proj_part)
    core = lax.axis_index("tok") % 2
    by_core = proj_part.reshape(n_tok // 2, 2, share, slots)
    mine = lax.dynamic_index_in_dim(by_core, core, 1, keepdims=False)
    other = lax.dynamic_index_in_dim(by_core, 1 - core, 1, keepdims=False)
    mine = mine + swap(other.astype(BF16), "tok", 1).astype(F32)
    place = lax.axis_index("tok") // 2
    grad_proj = lax.dynamic_index_in_dim(mine, place, 0, keepdims=False)
    for k in range(1, n_tok // 2):
        sent = lax.dynamic_index_in_dim(mine, place ^ k, 0, keepdims=False).astype(BF16)
        grad_proj = grad_proj + swap(sent, "tok", 2 * k).astype(F32)
    return (grad_tokens, grad_proj, grad_weight_in, grad_weight_out)


def solution(mesh):
    return jax.shard_map(
        local,
        mesh=mesh,
        in_specs=(
            P("tok", "exp"),
            P("tok", "exp"),
            P(None, "exp"),
            P("exp", None, "tok"),
            P("exp", "tok", None),
            P("exp"),
            P("tok"),
        ),
        out_specs=(P("tok", "exp"), P("tok", "exp"), P("exp", None, "tok"), P("exp", "tok", None)),
        check_vma=False,
    )
```

```python
import functools

import jax
import jax.numpy as jnp
from jax import lax
from jax.experimental import pallas as pl
from jax.experimental.pallas import tpu as pltpu
from jax.sharding import PartitionSpec as P

GELU_C = 0.7978845608028654
BF16 = jnp.bfloat16
F16 = jnp.float16
F32 = jnp.float32
LANES = 128
MIB = 1024 * 1024


def gelu_parts(pre_act):
    square = pre_act * pre_act
    tangent = jnp.tanh(GELU_C * (pre_act + 0.044715 * (square * pre_act)))
    value = 0.5 * pre_act * (1.0 + tangent)
    slope = 0.5 * (1.0 + tangent) + 0.5 * pre_act * (1.0 - tangent * tangent) * GELU_C * (
        1.0 + 3.0 * 0.044715 * square
    )
    return (value, slope)


def dot(a, b, ca, cb):
    return lax.dot_general(a, b, (((ca,), (cb,)), ((), ())), preferred_element_type=F32)


def swap(x, axis, k):
    n = lax.axis_size(axis)
    return lax.ppermute(x, axis, [(i, i ^ k) for i in range(n)])


def tree_of(n):
    def parent(k):
        bits = [b for b in (1 << i for i in range(n.bit_length())) if k & b]
        return k - (bits[1] if len(bits) > 2 else bits[0])

    def depth(k):
        return 1 + depth(parent(k)) if k else 0

    return {k: parent(k) for k in sorted(range(1, n), key=lambda k: (depth(k), -k))}


def gather_exp(block):
    tree = tree_of(lax.axis_size("exp"))
    held = {0: block}
    for k, source in tree.items():
        held[k] = swap(held[source], "exp", k ^ source)
    return [held[k] for k in range(len(held))]


def scatter_exp(blocks):
    tree = tree_of(lax.axis_size("exp"))
    for k, target in reversed(tree.items()):
        blocks[target] = blocks[target] + swap(blocks[k].astype(BF16), "exp", k ^ target).astype(F32)
    return blocks[0]


def to_half(x):
    top = jnp.maximum(jnp.max(jnp.abs(x), axis=1, keepdims=True), 1e-30)
    power = jnp.floor(jnp.log2(top))
    scaled = (x * jnp.exp2(14.0 - power)).astype(F16)
    return jnp.concatenate([scaled, jnp.broadcast_to(power.astype(F16), (x.shape[0], LANES))], axis=1)


def from_half(sent):
    return sent[:, :-LANES].astype(F32) * jnp.exp2(sent[:, -1:].astype(F32) - 14.0)


def call(body, outs, args, flops, scratch=(), waits=0, vmem=48):
    in_specs = [pl.BlockSpec(memory_space=pltpu.SMEM)]
    in_specs += [pl.BlockSpec(memory_space=pltpu.VMEM)] * (len(args) - 1 - waits)
    in_specs += [pl.BlockSpec(memory_space=pl.ANY)] * waits
    size = sum(a.size * a.dtype.itemsize for a in args) + sum(
        o.size * o.dtype.itemsize for o in outs
    )
    return pl.pallas_call(
        body,
        out_shape=outs,
        in_specs=in_specs,
        out_specs=[pl.BlockSpec(memory_space=pltpu.VMEM)] * len(outs),
        scratch_shapes=list(scratch),
        compiler_params=pltpu.CompilerParams(vmem_limit_bytes=vmem * MIB),
        cost_estimate=pl.CostEstimate(flops=flops, bytes_accessed=size, transcendentals=0),
    )(*args)


def sds(shape, dtype):
    return jax.ShapeDtypeStruct(shape, dtype)


def add_kernel(ours, got, *refs):
    refs[-1][...] = (ours[...] + got[...].astype(F32)).astype(refs[-1].dtype)


def add(ours, got, dtype, waits=()):
    if not waits:
        return (ours + got.astype(F32)).astype(dtype)
    corners = [corner(w) for w in waits]
    return pl.pallas_call(
        add_kernel,
        out_shape=sds(ours.shape, dtype),
        in_specs=[pl.BlockSpec(memory_space=pltpu.VMEM)] * (2 + len(corners)),
        out_specs=pl.BlockSpec(memory_space=pltpu.VMEM),
        compiler_params=pltpu.CompilerParams(vmem_limit_bytes=8 * MIB),
        cost_estimate=pl.CostEstimate(flops=ours.size, bytes_accessed=10 * ours.size, transcendentals=0),
    )(ours, got, *corners)


def corner(x):
    return lax.slice(x, (0, 0), (min(16, x.shape[0]), LANES))


def gate_kernel(idx, *refs):
    for i in range(idx.shape[0]):
        refs[-1][i] = idx[i]


def gate(idx, waits):
    corners = [corner(w) for w in waits]
    return pl.pallas_call(
        gate_kernel,
        out_shape=sds(idx.shape, idx.dtype),
        in_specs=[pl.BlockSpec(memory_space=pltpu.SMEM)] + [pl.BlockSpec(memory_space=pltpu.VMEM)] * len(corners),
        out_specs=pl.BlockSpec(memory_space=pltpu.SMEM),
        compiler_params=pltpu.CompilerParams(vmem_limit_bytes=MIB),
    )(idx, *corners)


def sum_core(mine, other, waits=()):
    return add(mine, swap(other, "tok", 1), F32, waits)


def sum_chips(mine, fine=False, waits=()):
    sent = to_half(mine) if fine else mine.astype(BF16)
    steps = range(2, lax.axis_size("tok"), 2)
    for k in steps:
        got = swap(sent, "tok", k)
        last = k == steps[-1]
        mine = add(mine, from_half(got) if fine else got, BF16 if last else F32, waits if last else ())
    return mine, swap(mine, "tok", 1)


def put_halves(core, part, mine, other):
    half = mine.shape[0]
    mine[...] = part[pl.ds(pl.multiple_of(core * half, half), half), :]
    other[...] = part[pl.ds(pl.multiple_of((1 - core) * half, half), half), :].astype(other.dtype)


def join_halves(core, mine, other, out):
    half = mine.shape[0]
    out[pl.ds(pl.multiple_of(core * half, half), half), :] = mine[...]
    out[pl.ds(pl.multiple_of((1 - core) * half, half), half), :] = other[...]


def place_blocks(me, blocks, out):
    feat = blocks[0].shape[0]
    for k, block in enumerate(blocks):
        out[pl.ds(pl.multiple_of((me ^ k) * feat, 16), feat), :] = block[...]


def slot_in_kernel(n, scale, idx, *refs):
    blocks = refs[:n]
    proj, slot_norm = refs[n : n + 2]
    tok, logits, mine, other, part = refs[-5:]
    place_blocks(idx[0], blocks, tok)
    value = dot(proj[...], tok[...], 0, 0)
    logits[...] = value
    dispatch = (jnp.exp(value - slot_norm[...]) / scale).astype(BF16)
    part[...] = dot(dispatch, tok[...], 1, 1)
    put_halves(idx[1], part, mine, other)


def slot_grad_kernel(n, scale, idx, *refs):
    blocks = refs[:n]
    logits, token_norm, grad, mine, other, part = refs[n:]
    place_blocks(idx[0], blocks, grad)
    combine = (jnp.exp(logits[...] - token_norm[...]) / scale).astype(BF16)
    part[...] = dot(combine, grad[...], 1, 1)
    put_halves(idx[1], part, mine, other)


def forward_kernel(idx, got_mine, got_other, w_in, w_out, _, slot_in, hidden, slope, mine, other, part):
    join_halves(idx[1], got_mine, got_other, slot_in)
    value, rate = gelu_parts(dot(slot_in[...], w_in[...], 1, 0))
    slope[...] = rate
    hidden[...] = value.astype(BF16)
    part[...] = dot(hidden[...], w_out[...], 1, 0)
    put_halves(idx[1], part, mine, other)


def backward_kernel(idx, got_mine, got_other, w_in, w_out, slope, slot_grad, pre_grad, mine, other, part):
    join_halves(idx[1], got_mine, got_other, slot_grad)
    hidden_grad = dot(slot_grad[...], w_out[...], 1, 1)
    pre_grad[...] = (hidden_grad * slope[...]).astype(BF16)
    part[...] = dot(pre_grad[...], w_in[...], 1, 1)
    put_halves(idx[1], part, mine, other)


def comb_kernel(scale, idx, got_mine, got_other, grad, logits, token_norm, weighted, row_part, joined):
    join_halves(idx[1], got_mine, got_other, joined)
    combine = jnp.exp(logits[...] - token_norm[...]) / scale
    value = combine * dot(joined[...], grad[...], 1, 0)
    weighted[...] = value
    row_part[...] = jnp.sum(value, axis=0, keepdims=True)


def final_kernel(tok_scale, slot_scale, idx, got_mine, got_other, tok, logits, slot_norm, token_norm, weighted,
                 row_stat, slot_in, proj, logit_grad, *refs):
    *blocks, joined, term = refs
    join_halves(idx[1], got_mine, got_other, joined)
    in_grad = joined[...]
    combine = jnp.exp(logits[...] - token_norm[...]) / slot_scale
    dispatch = jnp.exp(logits[...] - slot_norm[...]) / tok_scale
    col_stat = jnp.sum(slot_in[...].astype(F32) * in_grad.astype(F32), axis=1, keepdims=True)
    disp_grad = dot(in_grad, tok[...], 1, 0)
    value = weighted[...] - combine * row_stat[...] + dispatch * (disp_grad - col_stat)
    half = value.astype(BF16)
    logit_grad[...] = half
    term[...] = dot(proj[...], half, 1, 0) + dot(in_grad, dispatch.astype(BF16), 0, 0)
    feat = blocks[0].shape[0]
    for k, block in enumerate(blocks):
        block[...] = term[pl.ds(pl.multiple_of((idx[0] ^ k) * feat, 16), feat), :].astype(block.dtype)


def weight_grad_kernel(left, right, _, out):
    out[...] = dot(left[...], right[...], 0, 0)


def weight_grad(left, right, wait):
    slots, rows = left.shape
    columns = right.shape[1]
    block = 256 if rows % 256 == 0 else rows
    return pl.pallas_call(
        weight_grad_kernel,
        out_shape=sds((rows, columns), F32),
        grid=(rows // block,),
        in_specs=[
            pl.BlockSpec((slots, block), lambda i: (0, i)),
            pl.BlockSpec((slots, columns), lambda i: (0, 0)),
            pl.BlockSpec(memory_space=pl.ANY),
        ],
        out_specs=pl.BlockSpec((block, columns), lambda i: (i, 0)),
        compiler_params=pltpu.CompilerParams(vmem_limit_bytes=16 * MIB),
        cost_estimate=pl.CostEstimate(
            flops=2 * slots * rows * columns, bytes_accessed=4 * rows * columns, transcendentals=0
        ),
    )(left, right, wait)


def local(tokens, out_grad, slot_proj, weight_in, weight_out, slot_norm, token_norm):
    n_exp = lax.axis_size("exp")
    n_tok = lax.axis_size("tok")
    me = lax.axis_index("exp")
    place = lax.axis_index("tok")
    rows, feat = tokens.shape
    width = feat * n_exp
    slots = slot_proj.shape[1]
    half = slots // 2
    idx = jnp.stack([me, place % 2]).astype(jnp.int32)
    w_in, w_out = weight_in[0], weight_out[0]
    hidden_units = w_in.shape[1]
    slot_norm = slot_norm[:, None]
    token_norm = token_norm[None, :]
    tok_scale = float(rows * n_tok)
    slot_scale = float(slots * n_exp)
    halves = [sds((half, width), F32), sds((half, width), BF16)]
    wide = [sds((half, width), F32)] * 2
    part = pltpu.VMEM((slots, width), F32)

    tok_blocks = gather_exp(tokens.T.astype(BF16))
    grad_blocks = gather_exp(out_grad.T.astype(BF16))
    macs = 2 * rows * width * slots
    tok, logits, mine, other = call(
        functools.partial(slot_in_kernel, n_exp, tok_scale),
        [sds((width, rows), BF16), sds((slots, rows), F32), *wide],
        [gate(idx, [grad_blocks[k] for k in (4,)]), *tok_blocks, slot_proj, slot_norm],
        2 * macs,
        [part],
        vmem=50,
    )
    mine = sum_core(mine, other, [grad_blocks[k] for k in ()])
    got_in = sum_chips(mine, True, [grad_blocks[k] for k in (5, 6)])
    grad, grad_mine, grad_other = call(
        functools.partial(slot_grad_kernel, n_exp, slot_scale),
        [sds((width, rows), BF16), *halves],
        [idx, *grad_blocks, logits, token_norm],
        macs,
        [part],
        vmem=48,
    )
    slot_in, hidden, slope, mine, other = call(
        forward_kernel,
        [sds((slots, width), BF16), sds((slots, hidden_units), BF16), sds((slots, hidden_units), F32), *halves],
        [idx, *got_in, w_in, w_out, grad_other],
        4 * slots * width * hidden_units,
        [part],
        1,
        vmem=24,
    )
    out_mine = sum_core(mine, other)
    got_grad = sum_chips(sum_core(grad_mine, grad_other))
    got_out = sum_chips(out_mine)
    weighted, row_stat = call(
        functools.partial(comb_kernel, slot_scale),
        [sds((slots, rows), F32), sds((1, rows), F32)],
        [idx, *got_out, grad, logits, token_norm],
        macs,
        [pltpu.VMEM((slots, width), BF16)],
        vmem=24,
    )
    k = 1
    while k < n_exp:
        row_stat = row_stat + swap(row_stat, "exp", k)
        k *= 2
    slot_grad, pre_grad, mine, other = call(
        backward_kernel,
        [sds((slots, width), BF16), sds((slots, hidden_units), BF16), *halves],
        [idx, *got_grad, w_in, w_out, slope],
        4 * slots * width * hidden_units,
        [part],
        vmem=24,
    )
    got_in_grad = sum_chips(sum_core(mine, other), waits=[row_stat])
    summed = {0, *tree_of(n_exp).values()}
    blocks = [sds((feat, rows), F32 if k in summed else BF16) for k in range(n_exp)]
    logit_grad, *blocks = call(
        functools.partial(final_kernel, tok_scale, slot_scale),
        [sds((slots, rows), BF16), *blocks],
        [idx, *got_in_grad, tok, logits, slot_norm, token_norm, weighted, row_stat, slot_in, slot_proj],
        3 * macs,
        [pltpu.VMEM((slots, width), BF16), pltpu.VMEM((width, rows), F32)],
        vmem=40,
    )
    grad_tokens = scatter_exp(blocks).T

    grad_weight_out = weight_grad(hidden, slot_grad, logit_grad)[None]
    grad_weight_in = weight_grad(slot_in, pre_grad, logit_grad)[None]
    share = width // n_tok
    by_core = dot(tok, logit_grad, 1, 1).reshape(n_tok // 2, 2, share, slots)
    core, chip = place % 2, place // 2
    mine = lax.dynamic_index_in_dim(by_core, core, 1, keepdims=False)
    other = lax.dynamic_index_in_dim(by_core, 1 - core, 1, keepdims=False)
    mine = mine + swap(other.astype(BF16), "tok", 1).astype(F32)
    grad_proj = lax.dynamic_index_in_dim(mine, chip, 0, keepdims=False)
    for k in range(1, n_tok // 2):
        sent = lax.dynamic_index_in_dim(mine, chip ^ k, 0, keepdims=False).astype(BF16)
        grad_proj = grad_proj + swap(sent, "tok", 2 * k).astype(F32)
    return (grad_tokens, grad_proj, grad_weight_in, grad_weight_out)


def solution(mesh):
    return jax.shard_map(
        local,
        mesh=mesh,
        in_specs=(
            P("tok", "exp"),
            P("tok", "exp"),
            P(None, "exp"),
            P("exp", None, "tok"),
            P("exp", "tok", None),
            P("exp"),
            P("tok"),
        ),
        out_specs=(P("tok", "exp"), P("tok", "exp"), P("exp", None, "tok"), P("exp", "tok", None)),
        check_vma=False,
    )
```

```python
import functools

import jax
import jax.numpy as jnp
from jax import lax
from jax.experimental import pallas as pl
from jax.experimental.pallas import tpu as pltpu
from jax.sharding import PartitionSpec as P

GELU_C = 0.7978845608028654
BF16 = jnp.bfloat16
F16 = jnp.float16
F32 = jnp.float32
LANES = 128
MIB = 1024 * 1024


def gelu_parts(pre_act):
    square = pre_act * pre_act
    tangent = jnp.tanh(GELU_C * (pre_act + 0.044715 * (square * pre_act)))
    value = 0.5 * pre_act * (1.0 + tangent)
    slope = 0.5 * (1.0 + tangent) + 0.5 * pre_act * (1.0 - tangent * tangent) * GELU_C * (
        1.0 + 3.0 * 0.044715 * square
    )
    return (value, slope)


def dot(a, b, ca, cb):
    return lax.dot_general(a, b, (((ca,), (cb,)), ((), ())), preferred_element_type=F32)


def swap(x, axis, k):
    n = lax.axis_size(axis)
    return lax.ppermute(x, axis, [(i, i ^ k) for i in range(n)])


def tree_of(n):
    def parent(k):
        bits = [b for b in (1 << i for i in range(n.bit_length())) if k & b]
        return k - (bits[1] if len(bits) > 2 else bits[0])

    def depth(k):
        return 1 + depth(parent(k)) if k else 0

    return {k: parent(k) for k in sorted(range(1, n), key=lambda k: (depth(k), -k))}


def gather_exp(block):
    tree = tree_of(lax.axis_size("exp"))
    held = {0: block}
    for k, source in tree.items():
        held[k] = swap(held[source], "exp", k ^ source)
    return [held[k] for k in range(len(held))]


def scatter_exp(blocks):
    tree = tree_of(lax.axis_size("exp"))
    for k, target in reversed(tree.items()):
        blocks[target] = blocks[target] + swap(blocks[k].astype(BF16), "exp", k ^ target).astype(F32)
    return blocks[0]


def to_half(x):
    top = jnp.maximum(jnp.max(jnp.abs(x), axis=1, keepdims=True), 1e-30)
    power = jnp.floor(jnp.log2(top))
    scaled = (x * jnp.exp2(14.0 - power)).astype(F16)
    return jnp.concatenate([scaled, jnp.broadcast_to(power.astype(F16), (x.shape[0], LANES))], axis=1)


def from_half(sent):
    return sent[:, :-LANES].astype(F32) * jnp.exp2(sent[:, -1:].astype(F32) - 14.0)


def call(body, outs, args, flops, scratch=(), waits=(), vmem=48):
    count = len(args)
    in_specs = [pl.BlockSpec(memory_space=pltpu.SMEM)]
    in_specs += [pl.BlockSpec(memory_space=pltpu.VMEM)] * (count - 1)
    in_specs += [pl.BlockSpec(memory_space=pl.ANY)] * len(waits)
    size = sum(a.size * a.dtype.itemsize for a in args) + sum(
        o.size * o.dtype.itemsize for o in outs
    )

    def kernel(*refs):
        body(*refs[:count], *refs[count + len(waits) :])

    return pl.pallas_call(
        kernel,
        out_shape=outs,
        in_specs=in_specs,
        out_specs=[pl.BlockSpec(memory_space=pltpu.VMEM)] * len(outs),
        scratch_shapes=list(scratch),
        compiler_params=pltpu.CompilerParams(vmem_limit_bytes=vmem * MIB),
        cost_estimate=pl.CostEstimate(flops=flops, bytes_accessed=size, transcendentals=0),
    )(*args, *[corner(w) for w in waits])


def sds(shape, dtype):
    return jax.ShapeDtypeStruct(shape, dtype)


def add_kernel(ours, got, *refs):
    refs[-1][...] = (ours[...] + got[...].astype(F32)).astype(refs[-1].dtype)


def add(ours, got, dtype, waits=()):
    if not waits:
        return (ours + got.astype(F32)).astype(dtype)
    corners = [corner(w) for w in waits]
    return pl.pallas_call(
        add_kernel,
        out_shape=sds(ours.shape, dtype),
        in_specs=[pl.BlockSpec(memory_space=pltpu.VMEM)] * (2 + len(corners)),
        out_specs=pl.BlockSpec(memory_space=pltpu.VMEM),
        compiler_params=pltpu.CompilerParams(vmem_limit_bytes=8 * MIB),
        cost_estimate=pl.CostEstimate(flops=ours.size, bytes_accessed=10 * ours.size, transcendentals=0),
    )(ours, got, *corners)


def corner(x):
    piece = lax.slice(x, (0, 0), (min(16, x.shape[0]), LANES))
    return piece.astype(F32) if x.dtype == F16 else piece


def sum_core(mine, other, waits=()):
    return add(mine, swap(other, "tok", 1), F32, waits)


def sum_chips(mine, sent, waits=()):
    steps = range(2, lax.axis_size("tok"), 2)
    for k in steps:
        last = k == steps[-1]
        got = swap(sent, "tok", k)
        got = from_half(got) if got.dtype == F16 else got
        mine = add(mine, got, BF16 if last else F32, waits if last else ())
    return mine, swap(mine, "tok", 1)


def put_halves(core, part, mine, other):
    half = mine.shape[0]
    mine[...] = part[pl.ds(pl.multiple_of(core * half, half), half), :]
    other[...] = part[pl.ds(pl.multiple_of((1 - core) * half, half), half), :].astype(other.dtype)


def join_halves(core, mine, other, out):
    half = mine.shape[0]
    out[pl.ds(pl.multiple_of(core * half, half), half), :] = mine[...]
    out[pl.ds(pl.multiple_of((1 - core) * half, half), half), :] = other[...]


def place_blocks(me, blocks, out):
    feat = blocks[0].shape[0]
    for k, block in enumerate(blocks):
        out[pl.ds(pl.multiple_of((me ^ k) * feat, 16), feat), :] = block[...]


def slot_in_kernel(n, scale, idx, *refs):
    blocks = refs[:n]
    proj, slot_norm = refs[n : n + 2]
    tok, logits, mine, other, part = refs[-5:]
    place_blocks(idx[0], blocks, tok)
    value = dot(proj[...], tok[...], 0, 0)
    logits[...] = value
    dispatch = (jnp.exp(value - slot_norm[...]) / scale).astype(BF16)
    part[...] = dot(dispatch, tok[...], 1, 1)
    put_halves(idx[1], part, mine, other)


def slot_grad_kernel(n, scale, idx, *refs):
    blocks = refs[:n]
    logits, token_norm, grad, mine, other, part = refs[n:]
    place_blocks(idx[0], blocks, grad)
    combine = (jnp.exp(logits[...] - token_norm[...]) / scale).astype(BF16)
    part[...] = dot(combine, grad[...], 1, 1)
    put_halves(idx[1], part, mine, other)


def forward_kernel(idx, got_mine, got_other, w_in, w_out, slot_in, hidden, slope, mine, other, part):
    join_halves(idx[1], got_mine, got_other, slot_in)
    value, rate = gelu_parts(dot(slot_in[...], w_in[...], 1, 0))
    slope[...] = rate
    hidden[...] = value.astype(BF16)
    part[...] = dot(hidden[...], w_out[...], 1, 0)
    put_halves(idx[1], part, mine, other)


def backward_kernel(idx, got_mine, got_other, w_in, w_out, slope, slot_grad, pre_grad, mine, other, part):
    join_halves(idx[1], got_mine, got_other, slot_grad)
    hidden_grad = dot(slot_grad[...], w_out[...], 1, 1)
    pre_grad[...] = (hidden_grad * slope[...]).astype(BF16)
    part[...] = dot(pre_grad[...], w_in[...], 1, 1)
    put_halves(idx[1], part, mine, other)


def comb_kernel(scale, idx, got_mine, got_other, grad, logits, token_norm, weighted, row_part, joined):
    join_halves(idx[1], got_mine, got_other, joined)
    combine = jnp.exp(logits[...] - token_norm[...]) / scale
    value = combine * dot(joined[...], grad[...], 1, 0)
    weighted[...] = value
    row_part[...] = jnp.sum(value, axis=0, keepdims=True)


def final_kernel(tok_scale, slot_scale, idx, got_mine, got_other, tok, logits, slot_norm, token_norm, weighted,
                 row_stat, slot_in, proj, logit_grad, *refs):
    *blocks, joined, term = refs
    join_halves(idx[1], got_mine, got_other, joined)
    in_grad = joined[...]
    combine = jnp.exp(logits[...] - token_norm[...]) / slot_scale
    dispatch = jnp.exp(logits[...] - slot_norm[...]) / tok_scale
    col_stat = jnp.sum(slot_in[...].astype(F32) * in_grad.astype(F32), axis=1, keepdims=True)
    disp_grad = dot(in_grad, tok[...], 1, 0)
    value = weighted[...] - combine * row_stat[...] + dispatch * (disp_grad - col_stat)
    half = value.astype(BF16)
    logit_grad[...] = half
    term[...] = dot(proj[...], half, 1, 0) + dot(in_grad, dispatch.astype(BF16), 0, 0)
    feat = blocks[0].shape[0]
    for k, block in enumerate(blocks):
        block[...] = term[pl.ds(pl.multiple_of((idx[0] ^ k) * feat, 16), feat), :].astype(block.dtype)


def weight_grad_kernel(left, right, _, out):
    out[...] = dot(left[...], right[...], 0, 0)


def weight_grad(left, right, wait):
    slots, rows = left.shape
    columns = right.shape[1]
    block = 256 if rows % 256 == 0 else rows
    return pl.pallas_call(
        weight_grad_kernel,
        out_shape=sds((rows, columns), F32),
        grid=(rows // block,),
        in_specs=[
            pl.BlockSpec((slots, block), lambda i: (0, i)),
            pl.BlockSpec((slots, columns), lambda i: (0, 0)),
            pl.BlockSpec(memory_space=pl.ANY),
        ],
        out_specs=pl.BlockSpec((block, columns), lambda i: (i, 0)),
        compiler_params=pltpu.CompilerParams(vmem_limit_bytes=16 * MIB),
        cost_estimate=pl.CostEstimate(
            flops=2 * slots * rows * columns, bytes_accessed=4 * rows * columns, transcendentals=0
        ),
    )(left, right, wait)


def local(tokens, out_grad, slot_proj, weight_in, weight_out, slot_norm, token_norm):
    n_exp = lax.axis_size("exp")
    n_tok = lax.axis_size("tok")
    me = lax.axis_index("exp")
    place = lax.axis_index("tok")
    rows, feat = tokens.shape
    width = feat * n_exp
    slots = slot_proj.shape[1]
    half = slots // 2
    idx = jnp.stack([me, place % 2]).astype(jnp.int32)
    w_in, w_out = weight_in[0], weight_out[0]
    hidden_units = w_in.shape[1]
    slot_norm = slot_norm[:, None]
    token_norm = token_norm[None, :]
    tok_scale = float(rows * n_tok)
    slot_scale = float(slots * n_exp)
    wide = [sds((half, width), F32)] * 2
    part = pltpu.VMEM((slots, width), F32)

    tok_blocks = gather_exp(tokens.T.astype(BF16))
    grad_blocks = gather_exp(out_grad.T.astype(BF16))
    macs = 2 * rows * width * slots
    tok, logits, mine, other = call(
        functools.partial(slot_in_kernel, n_exp, tok_scale),
        [sds((width, rows), BF16), sds((slots, rows), F32), *wide],
        [idx, *tok_blocks, slot_proj, slot_norm],
        2 * macs,
        [part],
        waits=[grad_blocks[k] for k in (4,)],
        vmem=50,
    )
    mine = sum_core(mine, other, [grad_blocks[k] for k in ()])
    got_in = sum_chips(mine, mine, [grad_blocks[k] for k in (1,2,5,6)])
    grad, grad_mine, grad_other = call(
        functools.partial(slot_grad_kernel, n_exp, slot_scale),
        [sds((width, rows), BF16), *wide],
        [idx, *grad_blocks, logits, token_norm],
        macs,
        [part],
        waits=[got_in[0]],
        vmem=48,
    )
    grad_mine = sum_core(grad_mine, grad_other)
    grad_sent = to_half(grad_mine)
    slot_in, hidden, slope, mine, other = call(
        forward_kernel,
        [sds((slots, width), BF16), sds((slots, hidden_units), BF16), sds((slots, hidden_units), F32), *wide],
        [idx, *got_in, w_in, w_out],
        4 * slots * width * hidden_units,
        [part],
        waits=[grad_sent],
        vmem=24,
    )
    out_mine = sum_core(mine, other)
    got_grad = sum_chips(grad_mine, grad_sent)
    got_out = sum_chips(out_mine, to_half(out_mine))
    weighted, row_stat = call(
        functools.partial(comb_kernel, slot_scale),
        [sds((slots, rows), F32), sds((1, rows), F32)],
        [idx, *got_out, grad, logits, token_norm],
        macs,
        [pltpu.VMEM((slots, width), BF16)],
        vmem=24,
    )
    k = 1
    while k < n_exp:
        row_stat = row_stat + swap(row_stat, "exp", k)
        k *= 2
    slot_grad, pre_grad, mine, other = call(
        backward_kernel,
        [sds((slots, width), BF16), sds((slots, hidden_units), BF16), *wide],
        [idx, *got_grad, w_in, w_out, slope],
        4 * slots * width * hidden_units,
        [part],
        vmem=24,
    )
    mine = sum_core(mine, other)
    got_in_grad = sum_chips(mine, to_half(mine), [row_stat])
    summed = {0, *tree_of(n_exp).values()}
    blocks = [sds((feat, rows), F32 if k in summed else BF16) for k in range(n_exp)]
    logit_grad, *blocks = call(
        functools.partial(final_kernel, tok_scale, slot_scale),
        [sds((slots, rows), BF16), *blocks],
        [idx, *got_in_grad, tok, logits, slot_norm, token_norm, weighted, row_stat, slot_in, slot_proj],
        3 * macs,
        [pltpu.VMEM((slots, width), BF16), pltpu.VMEM((width, rows), F32)],
        vmem=40,
    )
    grad_tokens = scatter_exp(blocks).T

    grad_weight_out = weight_grad(hidden, slot_grad, logit_grad)[None]
    grad_weight_in = weight_grad(slot_in, pre_grad, logit_grad)[None]
    share = width // n_tok
    by_core = dot(tok, logit_grad, 1, 1).reshape(n_tok // 2, 2, share, slots)
    core, chip = place % 2, place // 2
    mine = lax.dynamic_index_in_dim(by_core, core, 1, keepdims=False)
    other = lax.dynamic_index_in_dim(by_core, 1 - core, 1, keepdims=False)
    mine = mine + swap(other.astype(BF16), "tok", 1).astype(F32)
    grad_proj = lax.dynamic_index_in_dim(mine, chip, 0, keepdims=False)
    for k in range(1, n_tok // 2):
        sent = lax.dynamic_index_in_dim(mine, chip ^ k, 0, keepdims=False).astype(BF16)
        grad_proj = grad_proj + swap(sent, "tok", 2 * k).astype(F32)
    return (grad_tokens, grad_proj, grad_weight_in, grad_weight_out)


def solution(mesh):
    return jax.shard_map(
        local,
        mesh=mesh,
        in_specs=(
            P("tok", "exp"),
            P("tok", "exp"),
            P(None, "exp"),
            P("exp", None, "tok"),
            P("exp", "tok", None),
            P("exp"),
            P("tok"),
        ),
        out_specs=(P("tok", "exp"), P("tok", "exp"), P("exp", None, "tok"), P("exp", "tok", None)),
        check_vma=False,
    )
```

```python
import functools

import jax
import jax.numpy as jnp
from jax import lax
from jax.experimental import pallas as pl
from jax.experimental.pallas import tpu as pltpu
from jax.sharding import PartitionSpec as P

GELU_C = 0.7978845608028654
BF16 = jnp.bfloat16
F16 = jnp.float16
F32 = jnp.float32
LANES = 128
MIB = 1024 * 1024


def gelu_parts(pre_act):
    square = pre_act * pre_act
    tangent = jnp.tanh(GELU_C * (pre_act + 0.044715 * (square * pre_act)))
    value = 0.5 * pre_act * (1.0 + tangent)
    slope = 0.5 * (1.0 + tangent) + 0.5 * pre_act * (1.0 - tangent * tangent) * GELU_C * (
        1.0 + 3.0 * 0.044715 * square
    )
    return (value, slope)


def dot(a, b, ca, cb):
    return lax.dot_general(a, b, (((ca,), (cb,)), ((), ())), preferred_element_type=F32)


def swap(x, axis, k):
    n = lax.axis_size(axis)
    return lax.ppermute(x, axis, [(i, i ^ k) for i in range(n)])


def tree_of(n):
    def parent(k):
        bits = [b for b in (1 << i for i in range(n.bit_length())) if k & b]
        return k - (bits[1] if len(bits) > 2 else bits[0])

    def depth(k):
        return 1 + depth(parent(k)) if k else 0

    return {k: parent(k) for k in sorted(range(1, n), key=lambda k: (depth(k), -k))}


def gather_exp(block):
    tree = tree_of(lax.axis_size("exp"))
    held = {0: block}
    for k, source in tree.items():
        held[k] = swap(held[source], "exp", k ^ source)
    return [held[k] for k in range(len(held))]


def scatter_exp(blocks):
    tree = tree_of(lax.axis_size("exp"))
    for k, target in reversed(tree.items()):
        blocks[target] = blocks[target] + swap(blocks[k].astype(BF16), "exp", k ^ target).astype(F32)
    return blocks[0]


def to_half(x):
    top = jnp.maximum(jnp.max(jnp.abs(x), axis=1, keepdims=True), 1e-30)
    power = jnp.floor(jnp.log2(top))
    scaled = (x * jnp.exp2(14.0 - power)).astype(F16)
    return jnp.concatenate([scaled, jnp.broadcast_to(power.astype(F16), (x.shape[0], LANES))], axis=1)


def from_half(sent):
    return sent[:, :-LANES].astype(F32) * jnp.exp2(sent[:, -1:].astype(F32) - 14.0)


def call(body, outs, args, flops, scratch=(), waits=(), vmem=48):
    count = len(args)
    in_specs = [pl.BlockSpec(memory_space=pltpu.SMEM)]
    in_specs += [pl.BlockSpec(memory_space=pltpu.VMEM)] * (count - 1)
    in_specs += [pl.BlockSpec(memory_space=pl.ANY)] * len(waits)
    size = sum(a.size * a.dtype.itemsize for a in args) + sum(
        o.size * o.dtype.itemsize for o in outs
    )

    def kernel(*refs):
        body(*refs[:count], *refs[count + len(waits) :])

    return pl.pallas_call(
        kernel,
        out_shape=outs,
        in_specs=in_specs,
        out_specs=[pl.BlockSpec(memory_space=pltpu.VMEM)] * len(outs),
        scratch_shapes=list(scratch),
        compiler_params=pltpu.CompilerParams(vmem_limit_bytes=vmem * MIB),
        cost_estimate=pl.CostEstimate(flops=flops, bytes_accessed=size, transcendentals=0),
    )(*args, *[corner(w) for w in waits])


def sds(shape, dtype):
    return jax.ShapeDtypeStruct(shape, dtype)


def add_kernel(ours, got, *refs):
    refs[-1][...] = (ours[...] + got[...].astype(F32)).astype(refs[-1].dtype)


def add(ours, got, dtype, waits=()):
    if not waits:
        return (ours + got.astype(F32)).astype(dtype)
    corners = [corner(w) for w in waits]
    return pl.pallas_call(
        add_kernel,
        out_shape=sds(ours.shape, dtype),
        in_specs=[pl.BlockSpec(memory_space=pltpu.VMEM)] * (2 + len(corners)),
        out_specs=pl.BlockSpec(memory_space=pltpu.VMEM),
        compiler_params=pltpu.CompilerParams(vmem_limit_bytes=8 * MIB),
        cost_estimate=pl.CostEstimate(flops=ours.size, bytes_accessed=10 * ours.size, transcendentals=0),
    )(ours, got, *corners)


def corner(x):
    piece = lax.slice(x, (0, 0), (min(16, x.shape[0]), LANES))
    return piece.astype(F32) if x.dtype == F16 else piece


def sum_core(mine, other, waits=()):
    return add(mine, swap(other, "tok", 1), F32, waits)


def sum_chips(mine, sent, waits=()):
    steps = range(2, lax.axis_size("tok"), 2)
    for k in steps:
        last = k == steps[-1]
        got = swap(sent, "tok", k)
        got = from_half(got) if got.dtype == F16 else got
        mine = add(mine, got, BF16 if last else F32, waits if last else ())
    return mine, swap(mine, "tok", 1)


def put_halves(core, part, mine, other):
    half = mine.shape[0]
    mine[...] = part[pl.ds(pl.multiple_of(core * half, half), half), :]
    other[...] = part[pl.ds(pl.multiple_of((1 - core) * half, half), half), :].astype(other.dtype)


def join_halves(core, mine, other, out):
    half = mine.shape[0]
    out[pl.ds(pl.multiple_of(core * half, half), half), :] = mine[...]
    out[pl.ds(pl.multiple_of((1 - core) * half, half), half), :] = other[...]


def place_blocks(me, blocks, out):
    feat = blocks[0].shape[0]
    for k, block in enumerate(blocks):
        out[pl.ds(pl.multiple_of((me ^ k) * feat, 16), feat), :] = block[...]


def slot_in_kernel(n, scale, idx, *refs):
    blocks = refs[:n]
    proj, slot_norm = refs[n : n + 2]
    tok, logits, mine, other, part = refs[-5:]
    place_blocks(idx[0], blocks, tok)
    value = dot(proj[...], tok[...], 0, 0)
    logits[...] = value
    dispatch = (jnp.exp(value - slot_norm[...]) / scale).astype(BF16)
    part[...] = dot(dispatch, tok[...], 1, 1)
    put_halves(idx[1], part, mine, other)


def slot_grad_kernel(n, scale, idx, *refs):
    blocks = refs[:n]
    logits, token_norm, grad, mine, other, part = refs[n:]
    place_blocks(idx[0], blocks, grad)
    combine = (jnp.exp(logits[...] - token_norm[...]) / scale).astype(BF16)
    part[...] = dot(combine, grad[...], 1, 1)
    put_halves(idx[1], part, mine, other)


def forward_kernel(idx, got_mine, got_other, w_in, w_out, slot_in, hidden, slope, mine, other, part):
    join_halves(idx[1], got_mine, got_other, slot_in)
    value, rate = gelu_parts(dot(slot_in[...], w_in[...], 1, 0))
    slope[...] = rate
    hidden[...] = value.astype(BF16)
    part[...] = dot(hidden[...], w_out[...], 1, 0)
    put_halves(idx[1], part, mine, other)


def backward_kernel(idx, got_mine, got_other, w_in, w_out, slope, slot_grad, pre_grad, mine, other, part):
    join_halves(idx[1], got_mine, got_other, slot_grad)
    hidden_grad = dot(slot_grad[...], w_out[...], 1, 1)
    pre_grad[...] = (hidden_grad * slope[...]).astype(BF16)
    part[...] = dot(pre_grad[...], w_in[...], 1, 1)
    put_halves(idx[1], part, mine, other)


def comb_kernel(scale, idx, got_mine, got_other, grad, logits, token_norm, weighted, row_part, joined):
    join_halves(idx[1], got_mine, got_other, joined)
    combine = jnp.exp(logits[...] - token_norm[...]) / scale
    value = combine * dot(joined[...], grad[...], 1, 0)
    weighted[...] = value
    row_part[...] = jnp.sum(value, axis=0, keepdims=True)


def final_kernel(tok_scale, slot_scale, idx, got_mine, got_other, tok, logits, slot_norm, token_norm, weighted,
                 row_stat, slot_in, proj, logit_grad, *refs):
    *blocks, joined, term = refs
    join_halves(idx[1], got_mine, got_other, joined)
    in_grad = joined[...]
    combine = jnp.exp(logits[...] - token_norm[...]) / slot_scale
    dispatch = jnp.exp(logits[...] - slot_norm[...]) / tok_scale
    col_stat = jnp.sum(slot_in[...].astype(F32) * in_grad.astype(F32), axis=1, keepdims=True)
    disp_grad = dot(in_grad, tok[...], 1, 0)
    value = weighted[...] - combine * row_stat[...] + dispatch * (disp_grad - col_stat)
    half = value.astype(BF16)
    logit_grad[...] = half
    term[...] = dot(proj[...], half, 1, 0) + dot(in_grad, dispatch.astype(BF16), 0, 0)
    feat = blocks[0].shape[0]
    for k, block in enumerate(blocks):
        block[...] = term[pl.ds(pl.multiple_of((idx[0] ^ k) * feat, 16), feat), :].astype(block.dtype)


def weight_grad_kernel(left, right, _, out):
    out[...] = dot(left[...], right[...], 0, 0)


def weight_grad(left, right, wait):
    slots, rows = left.shape
    columns = right.shape[1]
    block = 256 if rows % 256 == 0 else rows
    return pl.pallas_call(
        weight_grad_kernel,
        out_shape=sds((rows, columns), F32),
        grid=(rows // block,),
        in_specs=[
            pl.BlockSpec((slots, block), lambda i: (0, i)),
            pl.BlockSpec((slots, columns), lambda i: (0, 0)),
            pl.BlockSpec(memory_space=pl.ANY),
        ],
        out_specs=pl.BlockSpec((block, columns), lambda i: (i, 0)),
        compiler_params=pltpu.CompilerParams(vmem_limit_bytes=16 * MIB),
        cost_estimate=pl.CostEstimate(
            flops=2 * slots * rows * columns, bytes_accessed=4 * rows * columns, transcendentals=0
        ),
    )(left, right, wait)


def local(tokens, out_grad, slot_proj, weight_in, weight_out, slot_norm, token_norm):
    n_exp = lax.axis_size("exp")
    n_tok = lax.axis_size("tok")
    me = lax.axis_index("exp")
    place = lax.axis_index("tok")
    rows, feat = tokens.shape
    width = feat * n_exp
    slots = slot_proj.shape[1]
    half = slots // 2
    idx = jnp.stack([me, place % 2]).astype(jnp.int32)
    w_in, w_out = weight_in[0], weight_out[0]
    hidden_units = w_in.shape[1]
    slot_norm = slot_norm[:, None]
    token_norm = token_norm[None, :]
    tok_scale = float(rows * n_tok)
    slot_scale = float(slots * n_exp)
    wide = [sds((half, width), F32)] * 2
    part = pltpu.VMEM((slots, width), F32)

    tok_blocks = gather_exp(tokens.T.astype(BF16))
    grad_blocks = gather_exp(out_grad.T.astype(BF16))
    macs = 2 * rows * width * slots
    tok, logits, mine, other = call(
        functools.partial(slot_in_kernel, n_exp, tok_scale),
        [sds((width, rows), BF16), sds((slots, rows), F32), *wide],
        [idx, *tok_blocks, slot_proj, slot_norm],
        2 * macs,
        [part],
        waits=[grad_blocks[k] for k in (4,)],
        vmem=50,
    )
    mine = sum_core(mine, other, [grad_blocks[k] for k in ()])
    got_in = sum_chips(mine, mine, [grad_blocks[k] for k in (1,2,5,6)])
    grad, grad_mine, grad_other = call(
        functools.partial(slot_grad_kernel, n_exp, slot_scale),
        [sds((width, rows), BF16), *wide],
        [idx, *grad_blocks, logits, token_norm],
        macs,
        [part],
        waits=[got_in[0]],
        vmem=48,
    )
    grad_mine = sum_core(grad_mine, grad_other)
    grad_sent = to_half(grad_mine)
    slot_in, hidden, slope, mine, other = call(
        forward_kernel,
        [sds((slots, width), BF16), sds((slots, hidden_units), BF16), sds((slots, hidden_units), F32), *wide],
        [idx, *got_in, w_in, w_out],
        4 * slots * width * hidden_units,
        [part],
        waits=[grad_sent],
        vmem=24,
    )
    out_mine = sum_core(mine, other)
    got_grad = sum_chips(grad_mine, grad_sent)
    got_out = sum_chips(out_mine, to_half(out_mine))
    weighted, row_stat = call(
        functools.partial(comb_kernel, slot_scale),
        [sds((slots, rows), F32), sds((1, rows), F32)],
        [idx, *got_out, grad, logits, token_norm],
        macs,
        [pltpu.VMEM((slots, width), BF16)],
        vmem=24,
    )
    inner = 1 << ((n_exp.bit_length() - 1) // 2)
    for peers in (range(1, inner), range(inner, n_exp, inner)):
        row_part = row_stat
        for k in peers:
            row_stat = row_stat + swap(row_part, "exp", k)
    slot_grad, pre_grad, mine, other = call(
        backward_kernel,
        [sds((slots, width), BF16), sds((slots, hidden_units), BF16), *wide],
        [idx, *got_grad, w_in, w_out, slope],
        4 * slots * width * hidden_units,
        [part],
        vmem=24,
    )
    mine = sum_core(mine, other)
    got_in_grad = sum_chips(mine, to_half(mine), [row_stat])
    summed = {0, *tree_of(n_exp).values()}
    blocks = [sds((feat, rows), F32 if k in summed else BF16) for k in range(n_exp)]
    logit_grad, *blocks = call(
        functools.partial(final_kernel, tok_scale, slot_scale),
        [sds((slots, rows), BF16), *blocks],
        [idx, *got_in_grad, tok, logits, slot_norm, token_norm, weighted, row_stat, slot_in, slot_proj],
        3 * macs,
        [pltpu.VMEM((slots, width), BF16), pltpu.VMEM((width, rows), F32)],
        vmem=40,
    )
    grad_tokens = scatter_exp(blocks).T

    grad_weight_out = weight_grad(hidden, slot_grad, logit_grad)[None]
    grad_weight_in = weight_grad(slot_in, pre_grad, logit_grad)[None]
    share = width // n_tok
    by_core = dot(tok, logit_grad, 1, 1).reshape(n_tok // 2, 2, share, slots)
    core, chip = place % 2, place // 2
    mine = lax.dynamic_index_in_dim(by_core, core, 1, keepdims=False)
    other = lax.dynamic_index_in_dim(by_core, 1 - core, 1, keepdims=False)
    mine = mine + swap(other.astype(BF16), "tok", 1).astype(F32)
    grad_proj = lax.dynamic_index_in_dim(mine, chip, 0, keepdims=False)
    for k in range(1, n_tok // 2):
        sent = lax.dynamic_index_in_dim(mine, chip ^ k, 0, keepdims=False).astype(BF16)
        grad_proj = grad_proj + swap(sent, "tok", 2 * k).astype(F32)
    return (grad_tokens, grad_proj, grad_weight_in, grad_weight_out)


def solution(mesh):
    return jax.shard_map(
        local,
        mesh=mesh,
        in_specs=(
            P("tok", "exp"),
            P("tok", "exp"),
            P(None, "exp"),
            P("exp", None, "tok"),
            P("exp", "tok", None),
            P("exp"),
            P("tok"),
        ),
        out_specs=(P("tok", "exp"), P("tok", "exp"), P("exp", None, "tok"), P("exp", "tok", None)),
        check_vma=False,
    )
```
